512 devices in a mesh: row: 64 (over y, z_lo, core), pair: 8 (over z_hi, x).
Axes of the slice: x: 4, y: 4, z: 16 (z_hi: 2, z_lo: 8; z = z_hi * 8 + z_lo), core: 2. Of those that a mesh axis runs over, the one named last changes fastest.
Arguments:
- matrix: float32 [32768, 8192], P('row', 'pair'), may hold values from -100 to 100
- rotations: float32 [2, 8, 1024, 1024], P(None, 'pair', 'row'), may hold values from -0.1875 to 0.1875
Outputs:
- rotated: float32 [32768, 8192], P('row', 'pair')
- coupling: float32 [2, 8, 512, 512], P(None, 'pair', 'row')
The draws below stay inside these ranges and needn't reach their ends.
All inputs are finite; a program needn't handle non-finite values.
Results may differ from the reference program's by a relative error of at most 0.00012.
Values sent between devices are 32-bit elements; how exact they have to be, the bound alone decides.
A program may use at most 64 MiB of HBM per device.

```python
import math
import jax
import jax.numpy as jnp
from jax import lax

B = 512
ROUNDS = 2
PAIRS = 8
COLS = 8192
ROWS = 32768


def draw_matrix(key, part):
    key = jax.random.fold_in(key, 11)
    first, second, third = jax.random.split(key, 3)
    index = jnp.arange(ROWS, dtype=jnp.float32)
    rise = jnp.exp(math.log(3.0) * index / max(ROWS - 1, 1)) / math.sqrt(3.0)
    row_scale = rise * jnp.exp(jax.random.uniform(first, (ROWS,), jnp.float32, math.log(0.3), math.log(3.0)))
    col_scale = jnp.exp(jax.random.uniform(second, (COLS,), jnp.float32, math.log(0.3), math.log(3.0)))
    base = jnp.clip(jax.random.normal(third, (ROWS, COLS), jnp.float32), -6.0, 6.0)
    return (base * row_scale[:, None] * col_scale[None, :]).astype(jnp.float32)


def shard_levels(stream_key, extent, cuts, low, high):
    gain = 1.0
    for axis_at, blocks in cuts:
        heights = jax.random.uniform(jax.random.fold_in(jax.random.fold_in(stream_key, 6), axis_at), (blocks,), jnp.float32, low / len(cuts), high / len(cuts))
        gain = gain * jnp.repeat(jnp.exp(heights), extent[axis_at] // blocks).reshape((-1,) + (1,) * (len(extent) - 1 - axis_at))
    return gain


def noise(key, shape, width, most, pieces=(), held_as=jnp.bfloat16):
    drawn = jax.random.normal(key, shape, jnp.float32) * width
    if len(pieces) > 0:
        drawn = shard_levels(key, shape, pieces, -0.22, 0.18) * drawn
    return jnp.clip(drawn, min=-most, max=most).astype(held_as)


def setup_inputs(seed: int = 0) -> dict:
    key_list = jax.random.split(jax.random.key(seed), 3)
    matrix = draw_matrix(jax.random.fold_in(key_list[2], 71), 0)
    rotations = noise(key_list[1], (ROUNDS, PAIRS, 2 * B, 2 * B), (2 * B) ** -0.5, 0.1875, ((1, 8), (2, 64)), jnp.float32)
    return {"matrix": matrix, "rotations": rotations}


HIGH = lax.Precision.HIGHEST

def reference(matrix, rotations):
    pairs = matrix.reshape(ROWS, PAIRS, 2 * B).transpose(1, 0, 2)
    tops = pairs[:, :, :B]
    bottoms = pairs[:, :, B:]
    couplings = []
    for step in range(ROUNDS):
        cross = jnp.einsum('pmi,pmj->pij', tops, bottoms, precision=HIGH)
        norm_top = lax.optimization_barrier(jnp.sum(tops * tops, axis=1))
        norm_bottom = lax.optimization_barrier(jnp.sum(bottoms * bottoms, axis=1))
        mean_top = norm_top / ROWS + 1e-06
        mean_bottom = norm_bottom / ROWS + 1e-06
        scale = jnp.sqrt(jnp.float32(ROWS)) * jnp.sqrt(mean_top[:, :, None] * mean_bottom[:, None, :])
        couplings.append(cross / scale)
        joined = jnp.concatenate([tops, bottoms], axis=2)
        turned = jnp.einsum('pmk,pkj->pmj', joined, rotations[step], precision=HIGH)
        tops = turned[:, :, :B]
        bottoms = turned[:, :, B:]
        if step + 1 < ROUNDS:
            new_tops = jnp.concatenate([tops[:1], bottoms[:1], tops[1:-1]], axis=0)
            new_bottoms = jnp.concatenate([bottoms[1:], tops[-1:]], axis=0)
            tops = new_tops
            bottoms = new_bottoms
    joined = jnp.concatenate([tops, bottoms], axis=2)
    rotated = joined.transpose(1, 0, 2).reshape(ROWS, COLS)
    return (rotated, jnp.stack(couplings))
```

```python
import jax
import jax.numpy as jnp
from jax import lax
from jax.experimental import pallas as pl
from jax.experimental.pallas import tpu as pltpu
from jax.sharding import PartitionSpec as P

MESH = pl.DeviceIdType.MESH
F32 = jnp.float32
BF16 = jnp.bfloat16

YS, ZS, CS = 4, 8, 2
PAIRS = 8
B = 512
W = 2 * B
ROWS = 512
TOTAL = 32768
SHARE = 16
GROUP = 256
OFFSETS = (0, 512, 256, 768)
HALF = 512


def split(value):
    high = value.astype(BF16)
    return high, (value - high.astype(F32)).astype(BF16)


def dot3(a_high, a_low, b_high, b_low, dims):
    dot = lambda a, b: lax.dot_general(a, b, (dims, ((), ())), preferred_element_type=F32)
    return dot(a_high, b_high) + (dot(a_low, b_high) + dot(a_high, b_low))


def body(
    x_hbm, rot_ref, out_ref, coup_ref,
    x_ref, xh, xl, rg, staged, new, nh, nl,
    cx, nrm, rc, rcn, pb, pn, ry, ryn, qz, rz,
    x_sem, gs, gr, ms, mr, rs_s, rs_r,
):
    row = lax.axis_index("row")
    pair = lax.axis_index("pair")
    y = row // (ZS * CS)
    z = (row // CS) % ZS
    c = row % CS
    chip = y * ZS + z

    def at(yy, zz, cc):
        return ((yy * ZS + zz) * CS + cc, pair)

    sibling = at(y, z, 1 - c)
    after = (row, (pair + 1) % PAIRS)
    before = (row, (pair + PAIRS - 1) % PAIRS)
    y_other = [at((y + j) % YS, z, c) for j in range(1, YS)]
    z_other = [at(y, (z + j) % ZS, c) for j in range(1, ZS)]
    z_group = [at(y, (z // 4) * 4 + (z + j) % 4, c) for j in range(1, 4)]
    z_across = at(y, (z + 4) % ZS, c)

    pending = []

    def send(src, dst, s_sem, r_sem, device):
        copy = pltpu.make_async_remote_copy(
            src_ref=src, dst_ref=dst, send_sem=s_sem, recv_sem=r_sem,
            device_id=device, device_id_type=MESH,
        )
        copy.start()
        pending.append(copy)
        return copy

    x_copy = pltpu.make_async_copy(x_hbm, x_ref, x_sem)
    x_copy.start()

    barrier = pltpu.get_barrier_semaphore()
    partners = [sibling, after, before] + y_other + z_other
    for device in partners:
        pl.semaphore_signal(barrier, inc=1, device_id=device, device_id_type=MESH)
    own = pl.ds(pl.multiple_of(c * SHARE, SHARE), SHARE)
    for k in range(2):
        rg[k, pl.ds(chip, 1), own, :] = rot_ref[k]
    pl.semaphore_wait(barrier, len(partners))

    units = [(0, o, GROUP) for o in OFFSETS] + [(1, 0, HALF), (1, HALF, HALF)]
    waits = {}

    def gather_z1(u):
        k, o, n = units[u]
        ref = rg.at[k, pl.ds(chip, 1), own, pl.ds(o, n)]
        waits[u, "across"] = send(ref, ref, gs.at[u, 0], gr.at[u, 0], z_across)
        waits[u, "z1"] = [
            send(ref, ref, gs.at[u, 1 + j], gr.at[u, 1 + j], z_group[j]) for j in range(3)
        ]

    def gather_z2(u):
        k, o, n = units[u]
        waits[u, "across"].wait_recv()
        ref = rg.at[k, pl.ds(y * ZS + (z + 4) % ZS, 1), own, pl.ds(o, n)]
        waits[u, "z2"] = [
            send(ref, ref, gs.at[u, 4 + j], gr.at[u, 4 + j], z_group[j]) for j in range(3)
        ]

    def gather_y(u):
        k, o, n = units[u]
        for copy in waits[u, "z1"] + waits[u, "z2"]:
            copy.wait_recv()
        ref = rg.at[k, pl.ds(y * ZS, ZS), own, pl.ds(o, n)]
        waits[u, "y"] = [
            send(ref, ref, gs.at[u, 7 + j], gr.at[u, 7 + j], y_other[j]) for j in range(3)
        ]

    def gather_c(u):
        k, o, n = units[u]
        for copy in waits[u, "y"]:
            copy.wait_recv()
        ref = rg.at[k, :, own, pl.ds(o, n)]
        waits[u, "c"] = send(ref, ref, gs.at[u, 10], gr.at[u, 10], sibling)

    def gather_done(u):
        waits[u, "c"].wait_recv()

    def gram(k, high, low, top, bottom):
        for t in range(2):
            cols = slice(t * GROUP, (t + 1) * GROUP)
            tile = dot3(high[:, cols], low[:, cols], high[:, B:], low[:, B:], ((0,), (0,)))
            cx[k, 2 * t : 2 * t + 2] = tile.reshape(2, ZS, CS * 8, B)
        for i, ref in enumerate((top, bottom)):
            def add(step, total):
                part = ref[pl.ds(pl.multiple_of(step * 32, 32), 32), :]
                return total + jnp.sum((part * part).reshape(4, 8, B), axis=0)
            total = lax.fori_loop(0, ROWS // 32, add, jnp.zeros((8, B), F32))
            norm = jnp.sum(total, axis=0, keepdims=True)
            for j in range(4):
                nrm[k, 4 * i + j : 4 * i + j + 1, :] = norm[:, 128 * j : 128 * (j + 1)]

    mine = pl.ds(pl.multiple_of(c * 8, 8), 8)
    theirs = pl.ds(pl.multiple_of((1 - c) * 8, 8), 8)

    def reduce_c(k):
        waits[k, "rc"] = [
            send(cx.at[k, :, :, theirs, :], rc.at[k], rs_s.at[k, 0], rs_r.at[k, 0], sibling),
            send(nrm.at[k], rcn.at[k], rs_s.at[k, 1], rs_r.at[k, 1], sibling),
        ]

    def reduce_y(k):
        for copy in waits[k, "rc"]:
            copy.wait_recv()
        pb[k] = cx[k, :, :, mine, :] + rc[k]
        pn[k] = nrm[k] + rcn[k]
        waits[k, "ry"] = []
        for j in range(3):
            waits[k, "ry"] += [
                send(pb.at[k, (y + j + 1) % YS], ry.at[k, j], rs_s.at[k, 2 + j], rs_r.at[k, 2 + j], y_other[j]),
                send(pn.at[k], ryn.at[k, j], rs_s.at[k, 5 + j], rs_r.at[k, 5 + j], y_other[j]),
            ]

    def reduce_z(k):
        for copy in waits[k, "ry"]:
            copy.wait_recv()
        qz[k, :, :, :B] = pb[k, y] + ry[k, 0] + (ry[k, 1] + ry[k, 2])
        norms = pn[k] + ryn[k, 0] + (ryn[k, 1] + ryn[k, 2])
        for j in range(ZS):
            qz[k, j, :, B:] = norms
        waits[k, "rz"] = [
            send(qz.at[k, (z + j + 1) % ZS], rz.at[k, j], rs_s.at[k, 8 + j], rs_r.at[k, 8 + j], z_other[j])
            for j in range(7)
        ]

    def couple(k):
        for copy in waits[k, "rz"]:
            copy.wait_recv()
        total = qz[k, z]
        for j in range(7):
            total = total + rz[k, j]
        cross = total[:, :B]
        norms = total[:, B:]
        rows = [jnp.concatenate([norms[4 * i + j : 4 * i + j + 1, :] for j in range(4)], axis=1) for i in range(2)]
        mean_top = rows[0] / TOTAL + 1e-06
        mean_bottom = rows[1] / TOTAL + 1e-06
        here = lax.broadcasted_iota(jnp.int32, (8, B), 0) + 8 * row
        column = lax.broadcasted_iota(jnp.int32, (8, B), 1)
        mean_top = jnp.sum(jnp.where(here == column, mean_top, 0.0), axis=1, keepdims=True)
        scale = jnp.sqrt(F32(TOTAL)) * jnp.sqrt(mean_top * mean_bottom)
        coup_ref[k, 0] = cross / scale

    def turn(k, high, low, o):
        w = rg[k, :, :, o : o + GROUP].reshape(W, GROUP)
        w_high, w_low = split(w)
        return dot3(high[...], low[...], w_high, w_low, ((1,), (0,)))

    def move(g):
        src = staged.at[g]
        cols = pl.ds((g // 2) * GROUP, GROUP)
        sems = ms.at[g], mr.at[g]
        if g % 2 == 0:
            @pl.when(pair == 0)
            def _():
                new[0, :, cols] = src[...]

            @pl.when(pair == PAIRS - 1)
            def _():
                new[1, :, cols] = src[...]

            @pl.when((pair > 0) & (pair < PAIRS - 1))
            def _():
                up(g).start()
        else:
            @pl.when(pair == 0)
            def _():
                up(g).start()

            @pl.when(pair > 0)
            def _():
                down(g).start()

    def up(g):
        h = g // 2
        return pltpu.make_async_remote_copy(
            src_ref=staged.at[g], dst_ref=new.at[0, :, pl.ds(h * GROUP, GROUP)],
            send_sem=ms.at[g], recv_sem=mr.at[2 * h], device_id=after, device_id_type=MESH,
        )

    def down(g):
        h = g // 2
        return pltpu.make_async_remote_copy(
            src_ref=staged.at[g], dst_ref=new.at[1, :, pl.ds(h * GROUP, GROUP)],
            send_sem=ms.at[g], recv_sem=mr.at[2 * h + 1], device_id=before, device_id_type=MESH,
        )

    def arrived(g):
        if g % 2 == 0:
            @pl.when(pair > 0)
            def _():
                up(g).wait_recv()
        else:
            @pl.when(pair < PAIRS - 1)
            def _():
                down(g).wait_recv()
        i, h = g % 2, g // 2
        cols = slice(h * GROUP, (h + 1) * GROUP)
        into = slice(i * B + h * GROUP, i * B + (h + 1) * GROUP)
        nh[:, into], nl[:, into] = split(new[i, :, cols])

    def sent(g):
        if g % 2 == 0:
            @pl.when((pair > 0) & (pair < PAIRS - 1))
            def _():
                up(g).wait_send()
        else:
            @pl.when(pair == 0)
            def _():
                up(g).wait_send()

            @pl.when(pair > 0)
            def _():
                down(g).wait_send()

    for u in range(4):
        gather_z1(u)
    x_copy.wait()
    xh[...], xl[...] = split(x_ref[...])
    gram(0, xh, xl, x_ref.at[:, :B], x_ref.at[:, B:])

    def first(g):
        gather_done(g)
        staged[g] = turn(0, xh, xl, OFFSETS[g])
        move(g)

    gather_z2(0)
    gather_z2(1)
    gather_y(0)
    gather_z2(2)
    gather_y(1)
    gather_z2(3)
    gather_c(0)
    gather_y(2)
    first(0)
    gather_c(1)
    gather_y(3)
    gather_z1(4)
    gather_z1(5)
    first(1)
    gather_c(2)
    gather_z2(4)
    first(2)
    gather_z2(5)
    gather_c(3)
    gather_y(4)
    first(3)
    reduce_c(0)
    gather_y(5)
    reduce_y(0)
    gather_c(4)
    reduce_z(0)
    gather_c(5)
    couple(0)
    gather_done(4)
    gather_done(5)

    for g in range(4):
        arrived(g)
    gram(1, nh, nl, new.at[0], new.at[1])
    reduce_c(1)

    def second(g):
        out_ref[:, OFFSETS[g] : OFFSETS[g] + GROUP] = turn(1, nh, nl, OFFSETS[g])

    second(0)
    reduce_y(1)
    second(1)
    second(2)
    reduce_z(1)
    second(3)
    couple(1)
    for copy in pending:
        copy.wait_send()
    for g in range(4):
        sent(g)


def per_device(matrix, rotations):
    vmem = pl.BlockSpec(memory_space=pltpu.VMEM)
    scratch = [
        pltpu.VMEM((ROWS, W), F32),
        pltpu.VMEM((ROWS, W), BF16),
        pltpu.VMEM((ROWS, W), BF16),
        pltpu.VMEM((2, YS * ZS, CS * SHARE, W), F32),
        pltpu.VMEM((4, ROWS, GROUP), F32),
        pltpu.VMEM((2, ROWS, B), F32),
        pltpu.VMEM((ROWS, W), BF16),
        pltpu.VMEM((ROWS, W), BF16),
        pltpu.VMEM((2, YS, ZS, CS * 8, B), F32),
        pltpu.VMEM((2, 8, 128), F32),
        pltpu.VMEM((2, YS, ZS, 8, B), F32),
        pltpu.VMEM((2, 8, 128), F32),
        pltpu.VMEM((2, YS, ZS, 8, B), F32),
        pltpu.VMEM((2, 8, 128), F32),
        pltpu.VMEM((2, 3, ZS, 8, B), F32),
        pltpu.VMEM((2, 3, 8, 128), F32),
        pltpu.VMEM((2, ZS, 8, B + 128), F32),
        pltpu.VMEM((2, 7, 8, B + 128), F32),
        pltpu.SemaphoreType.DMA,
        pltpu.SemaphoreType.DMA((6, 11)),
        pltpu.SemaphoreType.DMA((6, 11)),
        pltpu.SemaphoreType.DMA((4,)),
        pltpu.SemaphoreType.DMA((4,)),
        pltpu.SemaphoreType.DMA((2, 15)),
        pltpu.SemaphoreType.DMA((2, 15)),
    ]
    return pl.pallas_call(
        body,
        name="tournament",
        out_shape=(
            jax.ShapeDtypeStruct((ROWS, W), F32),
            jax.ShapeDtypeStruct((2, 1, 8, B), F32),
        ),
        in_specs=[pl.BlockSpec(memory_space=pl.ANY), vmem],
        out_specs=(vmem, vmem),
        scratch_shapes=scratch,
        compiler_params=pltpu.CompilerParams(
            collective_id=0, has_side_effects=True, vmem_limit_bytes=56 << 20
        ),
    )(matrix, rotations)


def solution(mesh):
    specs = (P("row", "pair"), P(None, "pair", "row", None))
    return jax.shard_map(
        per_device, mesh=mesh, in_specs=specs, out_specs=specs, check_vma=False
    )
```

```python
import jax
import jax.numpy as jnp
from jax import lax
from jax.experimental import pallas as pl
from jax.experimental.pallas import tpu as pltpu
from jax.sharding import PartitionSpec as P

MESH = pl.DeviceIdType.MESH
F32 = jnp.float32
BF16 = jnp.bfloat16

YS, ZS, CS = 4, 8, 2
PAIRS = 8
B = 512
W = 2 * B
ROWS = 512
TOTAL = 32768
SHARE = 16
GROUP = 256
OFFSETS = (0, 512, 256, 768)
HALF = 512
QUARTER = 128


def split(value):
    high = value.astype(BF16)
    return high, (value - high.astype(F32)).astype(BF16)


def dot3(a_high, a_low, b_high, b_low, dims):
    dot = lambda a, b: lax.dot_general(a, b, (dims, ((), ())), preferred_element_type=F32)
    return dot(a_high, b_high) + (dot(a_low, b_high) + dot(a_high, b_low))


def body(
    x_hbm, rot_ref, out_ref, coup_ref,
    x_ref, xh, xl, rg, staged, new, nh, nl,
    cx, nrm, rc, rcn, pb, pn, ry, ryn, qz, rz,
    passing, x_sem, gs, gr, ms, mr, rs_s, rs_r, cs, cr, ps, pr,
):
    row = lax.axis_index("row")
    pair = lax.axis_index("pair")
    y = row // (ZS * CS)
    z = (row // CS) % ZS
    c = row % CS
    chip = y * ZS + z

    def at(yy, zz, cc):
        return ((yy * ZS + zz) * CS + cc, pair)

    sibling = at(y, z, 1 - c)
    pair_other = [(row, (pair + j) % PAIRS) for j in range(1, PAIRS)]
    after, before = pair_other[0], pair_other[-1]
    y_other = [at((y + j) % YS, z, c) for j in range(1, YS)]
    z_other = [at(y, (z + j) % ZS, c) for j in range(1, ZS)]
    z_group = [at(y, (z // 4) * 4 + (z + j) % 4, c) for j in range(1, 4)]
    z_across = at(y, (z + 4) % ZS, c)

    pending = []

    def send(src, dst, s_sem, r_sem, device):
        copy = pltpu.make_async_remote_copy(
            src_ref=src, dst_ref=dst, send_sem=s_sem, recv_sem=r_sem,
            device_id=device, device_id_type=MESH,
        )
        copy.start()
        pending.append(copy)
        return copy

    x_copy = pltpu.make_async_copy(x_hbm, x_ref, x_sem)
    x_copy.start()

    barrier = pltpu.get_barrier_semaphore()
    partners = [sibling] + pair_other + y_other + z_other
    for device in partners:
        pl.semaphore_signal(barrier, inc=1, device_id=device, device_id_type=MESH)
    own = pl.ds(pl.multiple_of(c * SHARE, SHARE), SHARE)
    for k in range(2):
        rg[k, pl.ds(chip, 1), own, :] = rot_ref[k]
    pl.semaphore_wait(barrier, len(partners))

    units = [(0, o, GROUP) for o in OFFSETS] + [(1, 0, HALF), (1, HALF, HALF)]
    waits = {}

    def gather_z1(u):
        k, o, n = units[u]
        ref = rg.at[k, pl.ds(chip, 1), own, pl.ds(o, n)]
        waits[u, "across"] = send(ref, ref, gs.at[u, 0], gr.at[u, 0], z_across)
        waits[u, "z1"] = [
            send(ref, ref, gs.at[u, 1 + j], gr.at[u, 1 + j], z_group[j]) for j in range(3)
        ]

    def gather_z2(u):
        k, o, n = units[u]
        waits[u, "across"].wait_recv()
        ref = rg.at[k, pl.ds(y * ZS + (z + 4) % ZS, 1), own, pl.ds(o, n)]
        waits[u, "z2"] = [
            send(ref, ref, gs.at[u, 4 + j], gr.at[u, 4 + j], z_group[j]) for j in range(3)
        ]

    def gather_y1(u):
        k, o, n = units[u]
        for copy in waits[u, "z1"] + waits[u, "z2"]:
            copy.wait_recv()
        ref = rg.at[k, pl.ds(y * ZS, ZS), own, pl.ds(o, n)]
        waits[u, "y1"] = [
            send(ref, ref, gs.at[u, 7 + j], gr.at[u, 7 + j], y_other[2 * j]) for j in range(2)
        ]

    def gather_y2(u):
        k, o, n = units[u]
        waits[u, "y2"] = []
        for j in range(2):
            waits[u, "y1"][j].wait_recv()
            first = ((y + (3, 1)[j]) % YS) * ZS + j * (ZS // 2)
            ref = rg.at[k, pl.ds(first, ZS // 2), own, pl.ds(o, n)]
            waits[u, "y2"].append(send(ref, ref, gs.at[u, 9 + j], gr.at[u, 9 + j], y_other[2 * j]))

    def gather_c(u):
        k, o, n = units[u]
        for copy in waits[u, "y2"]:
            copy.wait_recv()
        ref = rg.at[k, :, own, pl.ds(o, n)]
        waits[u, "c"] = send(ref, ref, gs.at[u, 11], gr.at[u, 11], sibling)

    def gather_done(u):
        waits[u, "c"].wait_recv()

    def gram(k, high, low, top, bottom):
        for t in range(2):
            cols = slice(t * GROUP, (t + 1) * GROUP)
            tile = dot3(high[:, cols], low[:, cols], high[:, B:], low[:, B:], ((0,), (0,)))
            cx[k, 2 * t : 2 * t + 2] = tile.reshape(2, ZS, CS * 8, B)
        for i, ref in enumerate((top, bottom)):
            def add(step, total):
                part = ref[pl.ds(pl.multiple_of(step * 32, 32), 32), :]
                return total + jnp.sum((part * part).reshape(4, 8, B), axis=0)
            total = lax.fori_loop(0, ROWS // 32, add, jnp.zeros((8, B), F32))
            norm = jnp.sum(total, axis=0, keepdims=True)
            for j in range(4):
                nrm[k, 4 * i + j : 4 * i + j + 1, :] = norm[:, 128 * j : 128 * (j + 1)]

    mine = pl.ds(pl.multiple_of(c * 8, 8), 8)
    theirs = pl.ds(pl.multiple_of((1 - c) * 8, 8), 8)

    def reduce_c(k):
        waits[k, "rc"] = [
            send(cx.at[k, :, :, theirs, :], rc.at[k], rs_s.at[k, 0], rs_r.at[k, 0], sibling),
            send(nrm.at[k], rcn.at[k], rs_s.at[k, 1], rs_r.at[k, 1], sibling),
        ]

    def reduce_y(k):
        for copy in waits[k, "rc"]:
            copy.wait_recv()
        pb[k] = cx[k, :, :, mine, :] + rc[k]
        pn[k] = nrm[k] + rcn[k]
        waits[k, "ry"] = []
        for j in range(3):
            waits[k, "ry"] += [
                send(pb.at[k, (y + j + 1) % YS], ry.at[k, j], rs_s.at[k, 2 + j], rs_r.at[k, 2 + j], y_other[j]),
                send(pn.at[k], ryn.at[k, j], rs_s.at[k, 5 + j], rs_r.at[k, 5 + j], y_other[j]),
            ]

    def reduce_z(k):
        for copy in waits[k, "ry"]:
            copy.wait_recv()
        qz[k, :, :, :B] = pb[k, y] + ry[k, 0] + (ry[k, 1] + ry[k, 2])
        norms = pn[k] + ryn[k, 0] + (ryn[k, 1] + ryn[k, 2])
        for j in range(ZS):
            qz[k, j, :, B:] = norms
        waits[k, "rz"] = [
            send(qz.at[k, (z + j + 1) % ZS], rz.at[k, j], rs_s.at[k, 8 + j], rs_r.at[k, 8 + j], z_other[j])
            for j in range(7)
        ]

    def couple(k):
        for copy in waits[k, "rz"]:
            copy.wait_recv()
        total = qz[k, z]
        for j in range(7):
            total = total + rz[k, j]
        cross = total[:, :B]
        norms = total[:, B:]
        rows = [jnp.concatenate([norms[4 * i + j : 4 * i + j + 1, :] for j in range(4)], axis=1) for i in range(2)]
        mean_top = rows[0] / TOTAL + 1e-06
        mean_bottom = rows[1] / TOTAL + 1e-06
        here = lax.broadcasted_iota(jnp.int32, (8, B), 0) + 8 * row
        column = lax.broadcasted_iota(jnp.int32, (8, B), 1)
        mean_top = jnp.sum(jnp.where(here == column, mean_top, 0.0), axis=1, keepdims=True)
        scale = jnp.sqrt(F32(TOTAL)) * jnp.sqrt(mean_top * mean_bottom)
        coup_ref[k, 0] = cross / scale

    def turn(k, high, low, o):
        w = rg[k, :, :, o : o + GROUP].reshape(W, GROUP)
        w_high, w_low = split(w)
        return dot3(high[...], low[...], w_high, w_low, ((1,), (0,)))

    def is_up(g):
        if g % 2 == 1:
            return pair == 0
        return (pair > 0) & (pair < PAIRS - 1) & (pair != 3)

    def is_down(g):
        return (pair > 0) & (pair != 4) if g % 2 == 1 else None

    def move(g):
        src = staged.at[g]
        cols = pl.ds((g // 2) * GROUP, GROUP)

        @pl.when(is_up(g))
        def _():
            up(g).start()

        if g % 2 == 0:
            @pl.when(pair == 0)
            def _():
                new[0, :, cols] = src[...]

            @pl.when(pair == PAIRS - 1)
            def _():
                new[1, :, cols] = src[...]
        else:
            @pl.when(is_down(g))
            def _():
                down(g).start()

        @pl.when(pair == 3 + g % 2)
        def _():
            for j in range(4):
                far(g, j).start()

    def far(g, j):
        i, h = g % 2, g // 2
        rows = pl.ds(j * QUARTER, QUARTER)
        dst = new.at[i, rows, pl.ds(h * GROUP, GROUP)] if j == 0 else passing.at[h]
        to = 4 - i if j == 0 else (3 - j, 4 + j)[i]
        return pltpu.make_async_remote_copy(
            src_ref=staged.at[g, rows], dst_ref=dst, send_sem=cs.at[h, j],
            recv_sem=cr.at[h, 0] if j == 0 else pr.at[h], device_id=(row, to), device_id_type=MESH,
        )

    def passed(g, j):
        i, h = g % 2, g // 2
        return pltpu.make_async_remote_copy(
            src_ref=passing.at[h], dst_ref=new.at[i, pl.ds(j * QUARTER, QUARTER), pl.ds(h * GROUP, GROUP)],
            send_sem=ps.at[h], recv_sem=cr.at[h, j], device_id=(row, 4 - i), device_id_type=MESH,
        )

    def pass_on(g):
        for j in range(1, 4):
            @pl.when(pair == (3 - j, 4 + j)[g % 2])
            def _():
                far(g, j).wait_recv()
                passed(g, j).start()

    def up(g):
        h = g // 2
        return pltpu.make_async_remote_copy(
            src_ref=staged.at[g], dst_ref=new.at[0, :, pl.ds(h * GROUP, GROUP)],
            send_sem=ms.at[g], recv_sem=mr.at[2 * h], device_id=after, device_id_type=MESH,
        )

    def down(g):
        h = g // 2
        return pltpu.make_async_remote_copy(
            src_ref=staged.at[g], dst_ref=new.at[1, :, pl.ds(h * GROUP, GROUP)],
            send_sem=ms.at[g], recv_sem=mr.at[2 * h + 1], device_id=before, device_id_type=MESH,
        )

    def arrived(g):
        i, h = g % 2, g // 2
        if i == 0:
            @pl.when((pair > 0) & (pair != 4))
            def _():
                up(g).wait_recv()
        else:
            @pl.when((pair < PAIRS - 1) & (pair != 3))
            def _():
                down(g).wait_recv()

        @pl.when(pair == 4 - i)
        def _():
            far(g, 0).wait_recv()
            for j in range(1, 4):
                passed(g, j).wait_recv()

        cols = slice(h * GROUP, (h + 1) * GROUP)
        into = slice(i * B + h * GROUP, i * B + (h + 1) * GROUP)
        nh[:, into], nl[:, into] = split(new[i, :, cols])

    def sent(g):
        @pl.when(is_up(g))
        def _():
            up(g).wait_send()

        if g % 2 == 1:
            @pl.when(is_down(g))
            def _():
                down(g).wait_send()

        @pl.when(pair == 3 + g % 2)
        def _():
            for j in range(4):
                far(g, j).wait_send()

        for j in range(1, 4):
            @pl.when(pair == (3 - j, 4 + j)[g % 2])
            def _():
                passed(g, j).wait_send()

    def first(g):
        gather_done(g)
        staged[g] = turn(0, xh, xl, OFFSETS[g])
        move(g)

    def second(g):
        out_ref[:, OFFSETS[g] : OFFSETS[g] + GROUP] = turn(1, nh, nl, OFFSETS[g])

    gather_z1(0)
    gather_z1(1)
    x_copy.wait()
    xh[...], xl[...] = split(x_ref[...])
    gram(0, xh, xl, x_ref.at[:, :B], x_ref.at[:, B:])
    reduce_c(0)
    gather_z2(0)
    gather_z1(2)
    gather_z2(1)
    gather_z1(3)
    reduce_y(0)
    gather_y1(0)
    gather_z2(2)
    gather_y1(1)
    gather_z2(3)
    gather_y2(0)
    gather_y1(2)
    gather_z1(4)
    gather_z1(5)
    gather_c(0)
    gather_y2(1)
    gather_y1(3)
    first(0)
    gather_c(1)
    gather_y2(2)
    reduce_z(0)
    first(1)
    pass_on(0)
    gather_c(2)
    gather_y2(3)
    gather_z2(4)
    gather_z2(5)
    first(2)
    pass_on(1)
    gather_c(3)
    gather_y1(4)
    first(3)
    pass_on(2)
    gather_y2(4)
    gather_y1(5)
    pass_on(3)
    couple(0)
    arrived(0)
    gather_c(4)
    gather_y2(5)
    arrived(1)
    arrived(2)
    gather_c(5)
    arrived(3)
    gram(1, nh, nl, new.at[0], new.at[1])
    reduce_c(1)
    gather_done(4)
    second(0)
    reduce_y(1)
    second(2)
    gather_done(5)
    second(1)
    reduce_z(1)
    second(3)
    couple(1)
    for copy in pending:
        copy.wait_send()
    for g in range(4):
        sent(g)


def per_device(matrix, rotations):
    vmem = pl.BlockSpec(memory_space=pltpu.VMEM)
    scratch = [
        pltpu.VMEM((ROWS, W), F32),
        pltpu.VMEM((ROWS, W), BF16),
        pltpu.VMEM((ROWS, W), BF16),
        pltpu.VMEM((2, YS * ZS, CS * SHARE, W), F32),
        pltpu.VMEM((4, ROWS, GROUP), F32),
        pltpu.VMEM((2, ROWS, B), F32),
        pltpu.VMEM((ROWS, W), BF16),
        pltpu.VMEM((ROWS, W), BF16),
        pltpu.VMEM((2, YS, ZS, CS * 8, B), F32),
        pltpu.VMEM((2, 8, 128), F32),
        pltpu.VMEM((2, YS, ZS, 8, B), F32),
        pltpu.VMEM((2, 8, 128), F32),
        pltpu.VMEM((2, YS, ZS, 8, B), F32),
        pltpu.VMEM((2, 8, 128), F32),
        pltpu.VMEM((2, 3, ZS, 8, B), F32),
        pltpu.VMEM((2, 3, 8, 128), F32),
        pltpu.VMEM((2, ZS, 8, B + 128), F32),
        pltpu.VMEM((2, 7, 8, B + 128), F32),
        pltpu.VMEM((2, QUARTER, GROUP), F32),
        pltpu.SemaphoreType.DMA,
        pltpu.SemaphoreType.DMA((6, 12)),
        pltpu.SemaphoreType.DMA((6, 12)),
        pltpu.SemaphoreType.DMA((4,)),
        pltpu.SemaphoreType.DMA((4,)),
        pltpu.SemaphoreType.DMA((2, 15)),
        pltpu.SemaphoreType.DMA((2, 15)),
        pltpu.SemaphoreType.DMA((2, 4)),
        pltpu.SemaphoreType.DMA((2, 4)),
        pltpu.SemaphoreType.DMA((2,)),
        pltpu.SemaphoreType.DMA((2,)),
    ]
    return pl.pallas_call(
        body,
        name="tournament",
        out_shape=(
            jax.ShapeDtypeStruct((ROWS, W), F32),
            jax.ShapeDtypeStruct((2, 1, 8, B), F32),
        ),
        in_specs=[pl.BlockSpec(memory_space=pl.ANY), vmem],
        out_specs=(vmem, vmem),
        scratch_shapes=scratch,
        compiler_params=pltpu.CompilerParams(
            collective_id=0, has_side_effects=True, vmem_limit_bytes=56 << 20
        ),
    )(matrix, rotations)


def solution(mesh):
    specs = (P("row", "pair"), P(None, "pair", "row", None))
    return jax.shard_map(
        per_device, mesh=mesh, in_specs=specs, out_specs=specs, check_vma=False
    )
```

```python
import jax
import jax.numpy as jnp
from jax import lax
from jax.experimental import pallas as pl
from jax.experimental.pallas import tpu as pltpu
from jax.sharding import PartitionSpec as P

MESH = pl.DeviceIdType.MESH
F32 = jnp.float32
BF16 = jnp.bfloat16

YS, ZS, CS = 4, 8, 2
PAIRS = 8
B = 512
W = 2 * B
ROWS = 512
TOTAL = 32768
SHARE = 16
GROUP = 256
PART = 128
HALF = 512
SHARES = ((0, 144), (144, 112), (256, 112), (368, 144))


def split(value):
    high = value.astype(BF16)
    return high, (value - high.astype(F32)).astype(BF16)


def dot3(a_high, a_low, b_high, b_low, dims):
    dot = lambda a, b: lax.dot_general(a, b, (dims, ((), ())), preferred_element_type=F32)
    return dot(a_high, b_high) + (dot(a_low, b_high) + dot(a_high, b_low))


def body(
    x_hbm, rot_ref, out_ref, coup_ref,
    x_ref, xh, xl, rg, staged, new, nh, nl,
    cx, nrm, rc, rcn, pb, pn, ry, ryn, qz, rz,
    passing, x_sem, gs, gr, ms, mr, rs_s, rs_r, cs, cr, ps, pr,
):
    row = lax.axis_index("row")
    pair = lax.axis_index("pair")
    y = row // (ZS * CS)
    z = (row // CS) % ZS
    c = row % CS
    chip = y * ZS + z

    def at(yy, zz, cc):
        return ((yy * ZS + zz) * CS + cc, pair)

    sibling = at(y, z, 1 - c)
    pair_other = [(row, (pair + j) % PAIRS) for j in range(1, PAIRS)]
    after, before = pair_other[0], pair_other[-1]
    y_other = [at((y + j) % YS, z, c) for j in range(1, YS)]
    z_other = [at(y, (z + j) % ZS, c) for j in range(1, ZS)]
    z_group = [at(y, (z // 4) * 4 + (z + j) % 4, c) for j in range(1, 4)]
    z_across = at(y, (z + 4) % ZS, c)

    pending = []

    def send(src, dst, s_sem, r_sem, device):
        copy = pltpu.make_async_remote_copy(
            src_ref=src, dst_ref=dst, send_sem=s_sem, recv_sem=r_sem,
            device_id=device, device_id_type=MESH,
        )
        copy.start()
        pending.append(copy)
        return copy

    x_copy = pltpu.make_async_copy(x_hbm, x_ref, x_sem)
    x_copy.start()

    barrier = pltpu.get_barrier_semaphore()
    partners = [sibling] + pair_other + y_other + z_other
    for device in partners:
        pl.semaphore_signal(barrier, inc=1, device_id=device, device_id_type=MESH)
    own = pl.ds(pl.multiple_of(c * SHARE, SHARE), SHARE)
    for u in range(4):
        for i in range(2):
            first_column = i * B + u * PART
            rg[0, pl.ds(chip, 1), own, u * GROUP + i * PART : u * GROUP + (i + 1) * PART] = rot_ref[
                0, :, :, first_column : first_column + PART
            ]
    rg[1, pl.ds(chip, 1), own, :] = rot_ref[1]
    pl.semaphore_wait(barrier, len(partners))

    units = [(0, 0, PART), (0, PART, PART)] + [(0, g * GROUP, GROUP) for g in range(1, 4)]
    units += [(1, 0, HALF), (1, HALF, HALF)]
    narrow = 2
    waits = {}

    def gather_z1(u):
        k, o, n = units[u]
        ref = rg.at[k, pl.ds(chip, 1), own, pl.ds(o, n)]
        waits[u, "across"] = send(ref, ref, gs.at[u, 0], gr.at[u, 0], z_across)
        waits[u, "z1"] = [
            send(ref, ref, gs.at[u, 1 + j], gr.at[u, 1 + j], z_group[j]) for j in range(3)
        ]

    def gather_z2(u):
        k, o, n = units[u]
        waits[u, "across"].wait_recv()
        ref = rg.at[k, pl.ds(y * ZS + (z + 4) % ZS, 1), own, pl.ds(o, n)]
        waits[u, "z2"] = [
            send(ref, ref, gs.at[u, 4 + j], gr.at[u, 4 + j], z_group[j]) for j in range(3)
        ]

    def gather_y1(u):
        k, o, n = units[u]
        for copy in waits[u, "z1"] + waits[u, "z2"]:
            copy.wait_recv()
        ref = rg.at[k, pl.ds(y * ZS, ZS), own, pl.ds(o, n)]
        waits[u, "y1"] = [
            send(ref, ref, gs.at[u, 7 + j], gr.at[u, 7 + j], y_other[2 * j]) for j in range(2)
        ]
        if u < narrow:
            waits[u, "y2"] = waits[u, "y1"] + [send(ref, ref, gs.at[u, 9], gr.at[u, 9], y_other[1])]

    def gather_y2(u):
        k, o, n = units[u]
        waits[u, "y2"] = []
        for j in range(2):
            waits[u, "y1"][j].wait_recv()
            first = ((y + (3, 1)[j]) % YS) * ZS + j * (ZS // 2)
            ref = rg.at[k, pl.ds(first, ZS // 2), own, pl.ds(o, n)]
            waits[u, "y2"].append(send(ref, ref, gs.at[u, 9 + j], gr.at[u, 9 + j], y_other[2 * j]))

    def gather_c(u):
        k, o, n = units[u]
        for copy in waits[u, "y2"]:
            copy.wait_recv()
        ref = rg.at[k, :, own, pl.ds(o, n)]
        waits[u, "c"] = send(ref, ref, gs.at[u, 11], gr.at[u, 11], sibling)

    def gather_done(u):
        waits[u, "c"].wait_recv()

    def gram(k, high, low, o, n):
        tile = dot3(high[:, :B], low[:, :B], high[:, B + o : B + o + n], low[:, B + o : B + o + n], ((0,), (0,)))
        cx[k, :, :, :, o : o + n] = tile.reshape(YS, ZS, CS * 8, n)

    def norms(k, top, bottom):
        for i, ref in enumerate((top, bottom)):
            def add(step, total):
                part = ref[pl.ds(pl.multiple_of(step * 32, 32), 32), :]
                return total + jnp.sum((part * part).reshape(4, 8, B), axis=0)
            total = lax.fori_loop(0, ROWS // 32, add, jnp.zeros((8, B), F32))
            norm = jnp.sum(total, axis=0, keepdims=True)
            for j in range(4):
                nrm[k, 4 * i + j : 4 * i + j + 1, :] = norm[:, 128 * j : 128 * (j + 1)]

    mine = pl.ds(pl.multiple_of(c * 8, 8), 8)
    theirs = pl.ds(pl.multiple_of((1 - c) * 8, 8), 8)
    parts = [(0, 0, B), (1, 0, GROUP), (1, GROUP, GROUP)]

    def reduce_c(q):
        k, o, n = parts[q]
        cols = pl.ds(o, n)
        waits[q, "rc"] = [
            send(cx.at[k, :, :, theirs, cols], rc.at[k, :, :, :, cols], rs_s.at[q, 0], rs_r.at[q, 0], sibling)
        ]
        if o == 0:
            waits[q, "rc"].append(send(nrm.at[k], rcn.at[k], rs_s.at[q, 1], rs_r.at[q, 1], sibling))

    def reduce_y(q):
        k, o, n = parts[q]
        cols = pl.ds(o, n)
        for copy in waits[q, "rc"]:
            copy.wait_recv()
        pb[k, :, :, :, cols] = cx[k, :, :, mine, cols] + rc[k, :, :, :, cols]
        if o == 0:
            pn[k] = nrm[k] + rcn[k]
        waits[q, "ry"] = []
        for j in range(3):
            waits[q, "ry"].append(
                send(
                    pb.at[k, (y + j + 1) % YS, :, :, cols], ry.at[k, j, :, :, cols],
                    rs_s.at[q, 2 + j], rs_r.at[q, 2 + j], y_other[j],
                )
            )
            if o == 0:
                waits[q, "ry"].append(send(pn.at[k], ryn.at[k, j], rs_s.at[q, 5 + j], rs_r.at[q, 5 + j], y_other[j]))

    def reduce_z(q):
        k, o, n = parts[q]
        cols = pl.ds(o, n)
        for copy in waits[q, "ry"]:
            copy.wait_recv()
        get = lambda ref, j: ref[k, j, :, :, cols]
        qz[k, :, :, 128 + o : 128 + o + n] = get(pb, y) + get(ry, 0) + (get(ry, 1) + get(ry, 2))
        if o == 0:
            total = pn[k] + ryn[k, 0] + (ryn[k, 1] + ryn[k, 2])
            for j in range(ZS):
                qz[k, j, :, :128] = total
        with_norms = pl.ds(0, n + 128) if o == 0 else pl.ds(o + 128, n)
        waits[q, "rz"] = [
            send(
                qz.at[k, (z + j + 1) % ZS, :, with_norms], rz.at[k, j, :, with_norms],
                rs_s.at[q, 8 + j], rs_r.at[q, 8 + j], z_other[j],
            )
            for j in range(7)
        ]

    def couple(k):
        for q in range(3):
            if parts[q][0] == k:
                for copy in waits[q, "rz"]:
                    copy.wait_recv()
        total = qz[k, z]
        for j in range(7):
            total = total + rz[k, j]
        cross = total[:, 128:]
        norm = total[:, :128]
        rows = [jnp.concatenate([norm[4 * i + j : 4 * i + j + 1, :] for j in range(4)], axis=1) for i in range(2)]
        mean_top = rows[0] / TOTAL + 1e-06
        mean_bottom = rows[1] / TOTAL + 1e-06
        here = lax.broadcasted_iota(jnp.int32, (8, B), 0) + 8 * row
        column = lax.broadcasted_iota(jnp.int32, (8, B), 1)
        mean_top = jnp.sum(jnp.where(here == column, mean_top, 0.0), axis=1, keepdims=True)
        scale = jnp.sqrt(F32(TOTAL)) * jnp.sqrt(mean_top * mean_bottom)
        coup_ref[k, 0] = cross / scale

    def turn(k, high, low, o, n):
        w = rg[k, :, :, o : o + n].reshape(W, n)
        w_high, w_low = split(w)
        return dot3(high[...], low[...], w_high, w_low, ((1,), (0,)))

    tops_up = (pair > 0) & (pair < PAIRS - 1) & (pair != 3)
    bottoms_down = (pair > 0) & (pair != 4)

    def up(g, i):
        return pltpu.make_async_remote_copy(
            src_ref=staged.at[g, :, pl.ds(i * PART, PART)], dst_ref=new.at[0, :, pl.ds(g * PART, PART)],
            send_sem=ms.at[g, i], recv_sem=mr.at[g, 0], device_id=after, device_id_type=MESH,
        )

    def down(g):
        return pltpu.make_async_remote_copy(
            src_ref=staged.at[g, :, pl.ds(PART, PART)], dst_ref=new.at[1, :, pl.ds(g * PART, PART)],
            send_sem=ms.at[g, 1], recv_sem=mr.at[g, 1], device_id=before, device_id_type=MESH,
        )

    def far(g, i, j):
        rows = pl.ds(*SHARES[j])
        return pltpu.make_async_remote_copy(
            src_ref=staged.at[g, rows, pl.ds(i * PART, PART)],
            dst_ref=new.at[i, rows, pl.ds(g * PART, PART)] if j == 0 else passing.at[g, pl.ds(0, SHARES[j][1])],
            send_sem=cs.at[g, j], recv_sem=cr.at[g, 0] if j == 0 else pr.at[g],
            device_id=(row, 4 - i if j == 0 else (3 - j, 4 + j)[i]), device_id_type=MESH,
        )

    def passed(g, i, j):
        return pltpu.make_async_remote_copy(
            src_ref=passing.at[g, pl.ds(0, SHARES[j][1])], dst_ref=new.at[i, pl.ds(*SHARES[j]), pl.ds(g * PART, PART)],
            send_sem=ps.at[g], recv_sem=cr.at[g, j], device_id=(row, 4 - i), device_id_type=MESH,
        )

    def move(g, i):
        @pl.when(pair == 3 + i)
        def _():
            for j in (1, 2, 3, 0):
                far(g, i, j).start()

        if i == 0:
            @pl.when(tops_up)
            def _():
                up(g, 0).start()
        else:
            @pl.when(pair == 0)
            def _():
                up(g, 1).start()

            @pl.when(bottoms_down)
            def _():
                down(g).start()

        if i == 0:
            for p in (0, PAIRS - 1):
                @pl.when(pair == p)
                def _():
                    new[p // (PAIRS - 1), :, g * PART : (g + 1) * PART] = staged[g, :, :PART]

    def pass_on(g):
        for i in range(2):
            for j in range(1, 4):
                @pl.when(pair == (3 - j, 4 + j)[i])
                def _():
                    far(g, i, j).wait_recv()
                    passed(g, i, j).start()

    def arrived(g):
        @pl.when((pair > 0) & (pair != 4))
        def _():
            up(g, 0).wait_recv()

        @pl.when((pair < PAIRS - 1) & (pair != 3))
        def _():
            down(g).wait_recv()

        for i in range(2):
            @pl.when(pair == 4 - i)
            def _():
                far(g, i, 0).wait_recv()
                for j in range(1, 4):
                    passed(g, i, j).wait_recv()

            cols = slice(g * PART, (g + 1) * PART)
            into = slice(i * B + g * PART, i * B + (g + 1) * PART)
            nh[:, into], nl[:, into] = split(new[i, :, cols])

    def sent(g):
        for i in range(2):
            @pl.when(pair == 3 + i)
            def _():
                for j in range(4):
                    far(g, i, j).wait_send()

            for j in range(1, 4):
                @pl.when(pair == (3 - j, 4 + j)[i])
                def _():
                    passed(g, i, j).wait_send()

        @pl.when(tops_up)
        def _():
            up(g, 0).wait_send()

        @pl.when(pair == 0)
        def _():
            up(g, 1).wait_send()

        @pl.when(bottoms_down)
        def _():
            down(g).wait_send()

    def first(u):
        gather_done(u)
        _, o, n = units[u]
        g, start = o // GROUP, o % GROUP
        staged[g, :, start : start + n] = turn(0, xh, xl, o, n)
        for i in range(start // PART, (start + n) // PART):
            move(g, i)

    def second(g):
        out_ref[:, g * GROUP : (g + 1) * GROUP] = turn(1, nh, nl, g * GROUP, GROUP)

    gather_z1(0)
    gather_z1(1)
    gather_z1(2)
    x_copy.wait()
    xh[...], xl[...] = split(x_ref[...])
    norms(0, x_ref.at[:, :B], x_ref.at[:, B:])
    gram(0, xh, xl, 0, B)
    reduce_c(0)
    gather_z2(0)
    gather_z2(1)
    gather_z1(3)
    gather_z1(4)
    gather_z2(2)
    gather_y1(0)
    gather_y1(1)
    gather_z2(3)
    gather_y1(2)
    gather_z2(4)
    gather_c(0)
    gather_c(1)
    gather_z1(5)
    gather_z1(6)
    gather_y2(2)
    gather_y1(3)
    first(0)
    first(1)
    gather_y1(4)
    gather_c(2)
    gather_y2(3)
    gather_z2(5)
    pass_on(0)
    first(2)
    gather_y2(4)
    reduce_y(0)
    gather_c(3)
    gather_z2(6)
    first(3)
    pass_on(1)
    gather_c(4)
    first(4)
    gather_y1(5)
    pass_on(2)
    pass_on(3)
    gather_y1(6)
    gather_y2(5)
    gather_y2(6)
    arrived(0)
    arrived(1)
    arrived(2)
    arrived(3)
    norms(1, new.at[0], new.at[1])
    gram(1, nh, nl, 0, GROUP)
    reduce_c(1)
    gram(1, nh, nl, GROUP, GROUP)
    reduce_c(2)
    gather_c(5)
    reduce_z(0)
    reduce_y(1)
    reduce_y(2)
    gather_c(6)
    gather_done(5)
    second(0)
    second(1)
    reduce_z(1)
    reduce_z(2)
    gather_done(6)
    second(2)
    second(3)
    couple(0)
    couple(1)
    for copy in pending:
        copy.wait_send()
    for g in range(4):
        sent(g)


def per_device(matrix, rotations):
    vmem = pl.BlockSpec(memory_space=pltpu.VMEM)
    scratch = [
        pltpu.VMEM((ROWS, W), F32),
        pltpu.VMEM((ROWS, W), BF16),
        pltpu.VMEM((ROWS, W), BF16),
        pltpu.VMEM((2, YS * ZS, CS * SHARE, W), F32),
        pltpu.VMEM((4, ROWS, GROUP), F32),
        pltpu.VMEM((2, ROWS, B), F32),
        pltpu.VMEM((ROWS, W), BF16),
        pltpu.VMEM((ROWS, W), BF16),
        pltpu.VMEM((2, YS, ZS, CS * 8, B), F32),
        pltpu.VMEM((2, 8, 128), F32),
        pltpu.VMEM((2, YS, ZS, 8, B), F32),
        pltpu.VMEM((2, 8, 128), F32),
        pltpu.VMEM((2, YS, ZS, 8, B), F32),
        pltpu.VMEM((2, 8, 128), F32),
        pltpu.VMEM((2, 3, ZS, 8, B), F32),
        pltpu.VMEM((2, 3, 8, 128), F32),
        pltpu.VMEM((2, ZS, 8, B + 128), F32),
        pltpu.VMEM((2, 7, 8, B + 128), F32),
        pltpu.VMEM((4, SHARES[0][1], PART), F32),
        pltpu.SemaphoreType.DMA,
        pltpu.SemaphoreType.DMA((7, 12)),
        pltpu.SemaphoreType.DMA((7, 12)),
        pltpu.SemaphoreType.DMA((4, 2)),
        pltpu.SemaphoreType.DMA((4, 2)),
        pltpu.SemaphoreType.DMA((3, 15)),
        pltpu.SemaphoreType.DMA((3, 15)),
        pltpu.SemaphoreType.DMA((4, 4)),
        pltpu.SemaphoreType.DMA((4, 4)),
        pltpu.SemaphoreType.DMA((4,)),
        pltpu.SemaphoreType.DMA((4,)),
    ]
    return pl.pallas_call(
        body,
        name="tournament",
        out_shape=(
            jax.ShapeDtypeStruct((ROWS, W), F32),
            jax.ShapeDtypeStruct((2, 1, 8, B), F32),
        ),
        in_specs=[pl.BlockSpec(memory_space=pl.ANY), vmem],
        out_specs=(vmem, vmem),
        scratch_shapes=scratch,
        compiler_params=pltpu.CompilerParams(
            collective_id=0, has_side_effects=True, vmem_limit_bytes=36 << 20
        ),
    )(matrix, rotations)


def solution(mesh):
    specs = (P("row", "pair"), P(None, "pair", "row", None))
    return jax.shard_map(
        per_device, mesh=mesh, in_specs=specs, out_specs=specs, check_vma=False
    )
```

```python
import jax
import jax.numpy as jnp
from jax import lax
from jax.experimental import pallas as pl
from jax.experimental.pallas import tpu as pltpu
from jax.sharding import PartitionSpec as P

MESH = pl.DeviceIdType.MESH
F32 = jnp.float32
BF16 = jnp.bfloat16

YS, ZS, CS = 4, 8, 2
PAIRS = 8
B = 512
W = 2 * B
ROWS = 512
TOTAL = 32768
SHARE = 16
GROUP = 256
PART = 128
HALF = 512
SHARES = ((0, 128), (128, 128), (256, 128), (384, 128))


def split(value):
    high = value.astype(BF16)
    return high, (value - high.astype(F32)).astype(BF16)


def dot3(a_high, a_low, b_high, b_low, dims):
    dot = lambda a, b: lax.dot_general(a, b, (dims, ((), ())), preferred_element_type=F32)
    return dot(a_high, b_high) + (dot(a_low, b_high) + dot(a_high, b_low))


def body(
    x_hbm, rot_ref, out_ref, coup_ref,
    x_ref, xh, xl, rg, staged, new, nh, nl,
    cx, nrm, rc, rcn, pb, pn, ry, ryn, qz, rz,
    passing, x_sem, gs, gr, ms, mr, rs_s, rs_r, cs, cr, ps, pr,
):
    row = lax.axis_index("row")
    pair = lax.axis_index("pair")
    y = row // (ZS * CS)
    z = (row // CS) % ZS
    c = row % CS
    chip = y * ZS + z

    def at(yy, zz, cc):
        return ((yy * ZS + zz) * CS + cc, pair)

    sibling = at(y, z, 1 - c)
    pair_other = [(row, (pair + j) % PAIRS) for j in range(1, PAIRS)]
    after, before = pair_other[0], pair_other[-1]
    y_other = [at((y + j) % YS, z, c) for j in range(1, YS)]
    z_other = [at(y, (z + j) % ZS, c) for j in range(1, ZS)]
    z_group = [at(y, (z // 4) * 4 + (z + j) % 4, c) for j in range(1, 4)]
    z_across = at(y, (z + 4) % ZS, c)

    pending = []

    def send(src, dst, s_sem, r_sem, device):
        copy = pltpu.make_async_remote_copy(
            src_ref=src, dst_ref=dst, send_sem=s_sem, recv_sem=r_sem,
            device_id=device, device_id_type=MESH,
        )
        copy.start()
        pending.append(copy)
        return copy

    x_copy = pltpu.make_async_copy(x_hbm, x_ref, x_sem)
    x_copy.start()

    barrier = pltpu.get_barrier_semaphore()
    partners = [sibling] + pair_other + y_other + z_other
    for device in partners:
        pl.semaphore_signal(barrier, inc=1, device_id=device, device_id_type=MESH)
    own = pl.ds(pl.multiple_of(c * SHARE, SHARE), SHARE)
    for p in range(8):
        i = jnp.where(pair == 3, p // 4, jnp.where(pair == 4, 1 - p // 4, p % 2))
        h = jnp.where((pair == 3) | (pair == 4), p % 4, p // 2)
        columns = pl.ds(pl.multiple_of(i * B + h * PART, PART), PART)
        rg[0, pl.ds(chip, 1), own, p * PART : (p + 1) * PART] = rot_ref[0, :, :, columns]
    rg[1, pl.ds(chip, 1), own, :] = rot_ref[1]
    pl.semaphore_wait(barrier, len(partners))

    units = [(0, 0, PART), (0, PART, PART)] + [(0, g * GROUP, GROUP) for g in range(1, 4)]
    units += [(1, 0, HALF), (1, HALF, HALF)]
    narrow = 2
    waits = {}

    def gather_z1(u):
        k, o, n = units[u]
        ref = rg.at[k, pl.ds(chip, 1), own, pl.ds(o, n)]
        waits[u, "across"] = send(ref, ref, gs.at[u, 0], gr.at[u, 0], z_across)
        waits[u, "z1"] = [
            send(ref, ref, gs.at[u, 1 + j], gr.at[u, 1 + j], z_group[j]) for j in range(3)
        ]

    def gather_z2(u):
        k, o, n = units[u]
        waits[u, "across"].wait_recv()
        ref = rg.at[k, pl.ds(y * ZS + (z + 4) % ZS, 1), own, pl.ds(o, n)]
        waits[u, "z2"] = [
            send(ref, ref, gs.at[u, 4 + j], gr.at[u, 4 + j], z_group[j]) for j in range(3)
        ]

    def gather_y1(u):
        k, o, n = units[u]
        for copy in waits[u, "z1"] + waits[u, "z2"]:
            copy.wait_recv()
        ref = rg.at[k, pl.ds(y * ZS, ZS), own, pl.ds(o, n)]
        waits[u, "y1"] = [
            send(ref, ref, gs.at[u, 7 + j], gr.at[u, 7 + j], y_other[2 * j]) for j in range(2)
        ]
        if u < narrow:
            waits[u, "y2"] = waits[u, "y1"] + [send(ref, ref, gs.at[u, 9], gr.at[u, 9], y_other[1])]

    def gather_y2(u):
        k, o, n = units[u]
        waits[u, "y2"] = []
        for j in range(2):
            waits[u, "y1"][j].wait_recv()
            first = ((y + (3, 1)[j]) % YS) * ZS + j * (ZS // 2)
            ref = rg.at[k, pl.ds(first, ZS // 2), own, pl.ds(o, n)]
            waits[u, "y2"].append(send(ref, ref, gs.at[u, 9 + j], gr.at[u, 9 + j], y_other[2 * j]))

    def gather_c(u):
        k, o, n = units[u]
        for copy in waits[u, "y2"]:
            copy.wait_recv()
        ref = rg.at[k, :, own, pl.ds(o, n)]
        waits[u, "c"] = send(ref, ref, gs.at[u, 11], gr.at[u, 11], sibling)

    def gather_done(u):
        waits[u, "c"].wait_recv()

    def gram(k, high, low, o, n):
        tile = dot3(high[:, :B], low[:, :B], high[:, B + o : B + o + n], low[:, B + o : B + o + n], ((0,), (0,)))
        cx[k, :, :, :, o : o + n] = tile.reshape(YS, ZS, CS * 8, n)

    def norms():
        for i in range(8):
            block = x_ref[:, i * PART : (i + 1) * PART]
            nrm[0, i : i + 1, :] = jnp.sum(block * block, axis=0, keepdims=True)

    mine = pl.ds(pl.multiple_of(c * 8, 8), 8)
    theirs = pl.ds(pl.multiple_of((1 - c) * 8, 8), 8)
    parts = [(0, 0, B), (1, 0, GROUP), (1, GROUP, GROUP)]

    def reduce_c(q):
        k, o, n = parts[q]
        cols = pl.ds(o, n)
        waits[q, "rc"] = [
            send(cx.at[k, :, :, theirs, cols], rc.at[k, :, :, :, cols], rs_s.at[q, 0], rs_r.at[q, 0], sibling)
        ]
        if o == 0:
            waits[q, "rc"].append(send(nrm.at[k], rcn.at[k], rs_s.at[q, 1], rs_r.at[q, 1], sibling))

    def reduce_y(q):
        k, o, n = parts[q]
        cols = pl.ds(o, n)
        for copy in waits[q, "rc"]:
            copy.wait_recv()
        pb[k, :, :, :, cols] = cx[k, :, :, mine, cols] + rc[k, :, :, :, cols]
        if o == 0:
            pn[k] = nrm[k] + rcn[k]
        waits[q, "ry"] = []
        for j in range(3):
            waits[q, "ry"].append(
                send(
                    pb.at[k, (y + j + 1) % YS, :, :, cols], ry.at[k, j, :, :, cols],
                    rs_s.at[q, 2 + j], rs_r.at[q, 2 + j], y_other[j],
                )
            )
            if o == 0:
                waits[q, "ry"].append(send(pn.at[k], ryn.at[k, j], rs_s.at[q, 5 + j], rs_r.at[q, 5 + j], y_other[j]))

    def reduce_z(q):
        k, o, n = parts[q]
        cols = pl.ds(o, n)
        for copy in waits[q, "ry"]:
            copy.wait_recv()
        get = lambda ref, j: ref[k, j, :, :, cols]
        qz[k, :, :, 128 + o : 128 + o + n] = get(pb, y) + get(ry, 0) + (get(ry, 1) + get(ry, 2))
        if o == 0:
            total = pn[k] + ryn[k, 0] + (ryn[k, 1] + ryn[k, 2])
            for j in range(ZS):
                qz[k, j, :, :128] = total
        with_norms = pl.ds(0, n + 128) if o == 0 else pl.ds(o + 128, n)
        waits[q, "rz"] = [
            send(
                qz.at[k, (z + j + 1) % ZS, :, with_norms], rz.at[k, j, :, with_norms],
                rs_s.at[q, 8 + j], rs_r.at[q, 8 + j], z_other[j],
            )
            for j in range(7)
        ]

    def couple(k):
        for q in range(3):
            if parts[q][0] == k:
                for copy in waits[q, "rz"]:
                    copy.wait_recv()
        total = qz[k, z]
        for j in range(7):
            total = total + rz[k, j]
        cross = total[:, 128:]
        norm = total[:, :128]
        rows = [jnp.concatenate([norm[4 * i + j : 4 * i + j + 1, :] for j in range(4)], axis=1) for i in range(2)]
        mean_top = rows[0] / TOTAL + 1e-06
        mean_bottom = rows[1] / TOTAL + 1e-06
        here = lax.broadcasted_iota(jnp.int32, (8, B), 0) + 8 * row
        column = lax.broadcasted_iota(jnp.int32, (8, B), 1)
        mean_top = jnp.sum(jnp.where(here == column, mean_top, 0.0), axis=1, keepdims=True)
        scale = jnp.sqrt(F32(TOTAL)) * jnp.sqrt(mean_top * mean_bottom)
        coup_ref[k, 0] = cross / scale

    def turn(k, high, low, o, n):
        w = rg[k, :, :, o : o + n].reshape(W, n)
        w_high, w_low = split(w)
        return dot3(high[...], low[...], w_high, w_low, ((1,), (0,)))

    plain = (pair != 3) & (pair != 4)
    tops_up = plain & (pair > 0) & (pair < PAIRS - 1)
    bottoms_down = plain & (pair > 0)

    def up(p, h):
        return pltpu.make_async_remote_copy(
            src_ref=staged.at[p], dst_ref=new.at[0, :, pl.ds(h * PART, PART)],
            send_sem=ms.at[p], recv_sem=mr.at[h, 0], device_id=after, device_id_type=MESH,
        )

    def down(p, h):
        return pltpu.make_async_remote_copy(
            src_ref=staged.at[p], dst_ref=new.at[1, :, pl.ds(h * PART, PART)],
            send_sem=ms.at[p], recv_sem=mr.at[h, 1], device_id=before, device_id_type=MESH,
        )

    def far(p, i, j):
        rows = pl.ds(*SHARES[j])
        return pltpu.make_async_remote_copy(
            src_ref=staged.at[p, rows],
            dst_ref=new.at[i, rows, pl.ds(p * PART, PART)] if j == 0 else passing.at[p, pl.ds(0, SHARES[j][1])],
            send_sem=cs.at[p, j], recv_sem=cr.at[p, 0] if j == 0 else pr.at[p],
            device_id=(row, 4 - i if j == 0 else (3 - j, 4 + j)[i]), device_id_type=MESH,
        )

    def passed(p, i, j):
        return pltpu.make_async_remote_copy(
            src_ref=passing.at[p, pl.ds(0, SHARES[j][1])], dst_ref=new.at[i, pl.ds(*SHARES[j]), pl.ds(p * PART, PART)],
            send_sem=ps.at[p], recv_sem=cr.at[p, j], device_id=(row, 4 - i), device_id_type=MESH,
        )

    def sends(p):
        i, h = p % 2, p // 2
        if p < 4:
            found = [(pair == 3 + k, [far(p, k, j) for j in (1, 2, 3, 0)]) for k in range(2)]
        else:
            found = [(pair == 3, [down(p, p - 4)]), (pair == 4, [up(p, p - 4)])]
        if i == 0:
            return found + [(tops_up, [up(p, h)])]
        return found + [(pair == 0, [up(p, h)]), (bottoms_down, [down(p, h)])]

    def move(p):
        for who, copies in sends(p):
            @pl.when(who)
            def _():
                for copy in copies:
                    copy.start()

        if p % 2 == 0:
            for k, at_pair in enumerate((0, PAIRS - 1)):
                @pl.when(pair == at_pair)
                def _():
                    new[k, :, p // 2 * PART : (p // 2 + 1) * PART] = staged[p]

    def sent(p):
        for who, copies in sends(p):
            @pl.when(who)
            def _():
                for copy in copies:
                    copy.wait_send()

        if p < 4:
            for i in range(2):
                for j in range(1, 4):
                    @pl.when(pair == (3 - j, 4 + j)[i])
                    def _():
                        passed(p, i, j).wait_send()

    def pass_on(p):
        for i in range(2):
            for j in range(1, 4):
                @pl.when(pair == (3 - j, 4 + j)[i])
                def _():
                    far(p, i, j).wait_recv()
                    passed(p, i, j).start()

    def arrived(h):
        @pl.when((pair > 0) & (pair != 4))
        def _():
            up(0, h).wait_recv()

        @pl.when((pair < PAIRS - 1) & (pair != 3))
        def _():
            down(0, h).wait_recv()

        for i in range(2):
            @pl.when(pair == 4 - i)
            def _():
                far(h, i, 0).wait_recv()
                for j in range(1, 4):
                    passed(h, i, j).wait_recv()

            into = slice(i * B + h * PART, i * B + (h + 1) * PART)
            block = new[i, :, h * PART : (h + 1) * PART]
            nh[:, into], nl[:, into] = split(block)
            nrm[1, 4 * i + h : 4 * i + h + 1, :] = jnp.sum(block * block, axis=0, keepdims=True)

    def first(u):
        gather_done(u)
        _, o, n = units[u]
        value = turn(0, xh, xl, o, n)
        for k in range(n // PART):
            staged[o // PART + k] = value[:, k * PART : (k + 1) * PART]
            move(o // PART + k)

    def second(g):
        out_ref[:, g * GROUP : (g + 1) * GROUP] = turn(1, nh, nl, g * GROUP, GROUP)

    gather_z1(0)
    gather_z1(1)
    gather_z1(2)
    x_copy.wait()
    xh[...], xl[...] = split(x_ref[...])
    norms()
    gram(0, xh, xl, 0, B)
    reduce_c(0)
    gather_z2(0)
    gather_z2(1)
    gather_z1(3)
    gather_z1(4)
    gather_z2(2)
    gather_y1(0)
    gather_y1(1)
    gather_z2(3)
    gather_y1(2)
    gather_z2(4)
    gather_z1(5)
    gather_z1(6)
    gather_c(0)
    gather_c(1)
    gather_y2(2)
    gather_y1(3)
    first(0)
    first(1)
    gather_y1(4)
    gather_c(2)
    gather_y2(3)
    pass_on(0)
    pass_on(1)
    gather_z2(5)
    first(2)
    gather_y2(4)
    reduce_y(0)
    gather_c(3)
    gather_z2(6)
    first(3)
    pass_on(2)
    pass_on(3)
    gather_c(4)
    first(4)
    gather_y1(5)
    gather_y1(6)
    arrived(0)
    arrived(1)
    arrived(2)
    arrived(3)
    gram(1, nh, nl, 0, GROUP)
    reduce_c(1)
    gram(1, nh, nl, GROUP, GROUP)
    reduce_c(2)
    reduce_y(1)
    reduce_y(2)
    gather_y2(5)
    gather_y2(6)
    reduce_z(0)
    reduce_z(1)
    reduce_z(2)
    gather_c(5)
    gather_c(6)
    gather_done(5)
    second(0)
    second(1)
    gather_done(6)
    second(2)
    second(3)
    couple(0)
    couple(1)
    for copy in pending:
        copy.wait_send()
    for p in range(8):
        sent(p)


def per_device(matrix, rotations):
    vmem = pl.BlockSpec(memory_space=pltpu.VMEM)
    scratch = [
        pltpu.VMEM((ROWS, W), F32),
        pltpu.VMEM((ROWS, W), BF16),
        pltpu.VMEM((ROWS, W), BF16),
        pltpu.VMEM((2, YS * ZS, CS * SHARE, W), F32),
        pltpu.VMEM((8, ROWS, PART), F32),
        pltpu.VMEM((2, ROWS, B), F32),
        pltpu.VMEM((ROWS, W), BF16),
        pltpu.VMEM((ROWS, W), BF16),
        pltpu.VMEM((2, YS, ZS, CS * 8, B), F32),
        pltpu.VMEM((2, 8, 128), F32),
        pltpu.VMEM((2, YS, ZS, 8, B), F32),
        pltpu.VMEM((2, 8, 128), F32),
        pltpu.VMEM((2, YS, ZS, 8, B), F32),
        pltpu.VMEM((2, 8, 128), F32),
        pltpu.VMEM((2, 3, ZS, 8, B), F32),
        pltpu.VMEM((2, 3, 8, 128), F32),
        pltpu.VMEM((2, ZS, 8, B + 128), F32),
        pltpu.VMEM((2, 7, 8, B + 128), F32),
        pltpu.VMEM((4, SHARES[0][1], PART), F32),
        pltpu.SemaphoreType.DMA,
        pltpu.SemaphoreType.DMA((7, 12)),
        pltpu.SemaphoreType.DMA((7, 12)),
        pltpu.SemaphoreType.DMA((8,)),
        pltpu.SemaphoreType.DMA((4, 2)),
        pltpu.SemaphoreType.DMA((3, 15)),
        pltpu.SemaphoreType.DMA((3, 15)),
        pltpu.SemaphoreType.DMA((4, 4)),
        pltpu.SemaphoreType.DMA((4, 4)),
        pltpu.SemaphoreType.DMA((4,)),
        pltpu.SemaphoreType.DMA((4,)),
    ]
    return pl.pallas_call(
        body,
        name="tournament",
        out_shape=(
            jax.ShapeDtypeStruct((ROWS, W), F32),
            jax.ShapeDtypeStruct((2, 1, 8, B), F32),
        ),
        in_specs=[pl.BlockSpec(memory_space=pl.ANY), vmem],
        out_specs=(vmem, vmem),
        scratch_shapes=scratch,
        compiler_params=pltpu.CompilerParams(
            collective_id=0, has_side_effects=True, vmem_limit_bytes=36 << 20
        ),
    )(matrix, rotations)


def solution(mesh):
    specs = (P("row", "pair"), P(None, "pair", "row", None))
    return jax.shard_map(
        per_device, mesh=mesh, in_specs=specs, out_specs=specs, check_vma=False
    )
```

```python
import jax
import jax.numpy as jnp
from jax import lax
from jax.experimental import pallas as pl
from jax.experimental.pallas import tpu as pltpu
from jax.sharding import PartitionSpec as P

MESH = pl.DeviceIdType.MESH
F32 = jnp.float32
BF16 = jnp.bfloat16

YS, ZS, CS = 4, 8, 2
PAIRS = 8
B = 512
W = 2 * B
ROWS = 512
TOTAL = 32768
SHARE = 16
GROUP = 256
PART = 128
HALF = 512
SHARES = ((0, 128), (128, 128), (256, 128), (384, 128))


def split(value):
    high = value.astype(BF16)
    return high, (value - high.astype(F32)).astype(BF16)


def dot3(a_high, a_low, b_high, b_low, dims):
    dot = lambda a, b: lax.dot_general(a, b, (dims, ((), ())), preferred_element_type=F32)
    return dot(a_high, b_high) + (dot(a_low, b_high) + dot(a_high, b_low))


def body(
    x_hbm, rot_ref, out_ref, coup_ref,
    x_ref, xh, xl, rg, staged, new, nh, nl,
    cx, nrm, rc, rcn, pb, pn, ry, ryn, qz, rz,
    passing, x_sem, gs, gr, ms, mr, rs_s, rs_r, cs, cr, ps, pr,
):
    row = lax.axis_index("row")
    pair = lax.axis_index("pair")
    y = row // (ZS * CS)
    z = (row // CS) % ZS
    c = row % CS
    chip = y * ZS + z

    def at(yy, zz, cc):
        return ((yy * ZS + zz) * CS + cc, pair)

    sibling = at(y, z, 1 - c)
    pair_other = [(row, (pair + j) % PAIRS) for j in range(1, PAIRS)]
    after, before = pair_other[0], pair_other[-1]
    y_other = [at((y + j) % YS, z, c) for j in range(1, YS)]
    z_other = [at(y, (z + j) % ZS, c) for j in range(1, ZS)]
    z_group = [at(y, (z // 4) * 4 + (z + j) % 4, c) for j in range(1, 4)]
    z_across = at(y, (z + 4) % ZS, c)

    pending = []

    def send(src, dst, s_sem, r_sem, device):
        copy = pltpu.make_async_remote_copy(
            src_ref=src, dst_ref=dst, send_sem=s_sem, recv_sem=r_sem,
            device_id=device, device_id_type=MESH,
        )
        copy.start()
        pending.append(copy)
        return copy

    x_copy = pltpu.make_async_copy(x_hbm, x_ref, x_sem)
    x_copy.start()

    barrier = pltpu.get_barrier_semaphore()
    partners = [sibling] + pair_other + y_other + z_other
    for device in partners:
        pl.semaphore_signal(barrier, inc=1, device_id=device, device_id_type=MESH)
    own = pl.ds(pl.multiple_of(c * SHARE, SHARE), SHARE)
    for p in range(8):
        i = jnp.where(pair == 3, p // 4, jnp.where(pair == 4, 1 - p // 4, p % 2))
        h = jnp.where((pair == 3) | (pair == 4), p % 4, p // 2)
        columns = pl.ds(pl.multiple_of(i * B + h * PART, PART), PART)
        rg[0, pl.ds(chip, 1), own, p * PART : (p + 1) * PART] = rot_ref[0, :, :, columns]
    rg[1, pl.ds(chip, 1), own, :] = rot_ref[1]
    pl.semaphore_wait(barrier, len(partners))

    units = [(0, 0, PART), (0, PART, PART)] + [(0, g * GROUP, GROUP) for g in range(1, 4)]
    units += [(1, 0, HALF), (1, HALF, HALF)]
    narrow = 2
    waits = {}

    def gather_z1(u):
        k, o, n = units[u]
        ref = rg.at[k, pl.ds(chip, 1), own, pl.ds(o, n)]
        waits[u, "across"] = send(ref, ref, gs.at[u, 0], gr.at[u, 0], z_across)
        waits[u, "z1"] = [
            send(ref, ref, gs.at[u, 1 + j], gr.at[u, 1 + j], z_group[j]) for j in range(3)
        ]

    def gather_z2(u):
        k, o, n = units[u]
        waits[u, "across"].wait_recv()
        ref = rg.at[k, pl.ds(y * ZS + (z + 4) % ZS, 1), own, pl.ds(o, n)]
        waits[u, "z2"] = [
            send(ref, ref, gs.at[u, 4 + j], gr.at[u, 4 + j], z_group[j]) for j in range(3)
        ]

    def gather_y1(u):
        k, o, n = units[u]
        for copy in waits[u, "z1"] + waits[u, "z2"]:
            copy.wait_recv()
        ref = rg.at[k, pl.ds(y * ZS, ZS), own, pl.ds(o, n)]
        waits[u, "y1"] = [
            send(ref, ref, gs.at[u, 7 + j], gr.at[u, 7 + j], y_other[2 * j]) for j in range(2)
        ]
        if u < narrow:
            waits[u, "y2"] = waits[u, "y1"] + [send(ref, ref, gs.at[u, 9], gr.at[u, 9], y_other[1])]

    def gather_y2(u):
        k, o, n = units[u]
        waits[u, "y2"] = []
        for j in range(2):
            waits[u, "y1"][j].wait_recv()
            first = ((y + (3, 1)[j]) % YS) * ZS + j * (ZS // 2)
            ref = rg.at[k, pl.ds(first, ZS // 2), own, pl.ds(o, n)]
            waits[u, "y2"].append(send(ref, ref, gs.at[u, 9 + j], gr.at[u, 9 + j], y_other[2 * j]))

    def gather_c(u):
        k, o, n = units[u]
        for copy in waits[u, "y2"]:
            copy.wait_recv()
        ref = rg.at[k, :, own, pl.ds(o, n)]
        waits[u, "c"] = send(ref, ref, gs.at[u, 11], gr.at[u, 11], sibling)

    def gather_done(u):
        waits[u, "c"].wait_recv()

    def gram(k, high, low, o, n):
        tile = dot3(high[:, :B], low[:, :B], high[:, B + o : B + o + n], low[:, B + o : B + o + n], ((0,), (0,)))
        cx[k, :, :, :, o : o + n] = tile.reshape(YS, ZS, CS * 8, n)

    def norms():
        for i in range(8):
            block = x_ref[:, i * PART : (i + 1) * PART]
            nrm[0, i : i + 1, :] = jnp.sum(block * block, axis=0, keepdims=True)

    mine = pl.ds(pl.multiple_of(c * 8, 8), 8)
    theirs = pl.ds(pl.multiple_of((1 - c) * 8, 8), 8)
    parts = [(0, 0, B), (1, 0, GROUP), (1, GROUP, GROUP)]

    def reduce_c(q):
        k, o, n = parts[q]
        cols = pl.ds(o, n)
        waits[q, "rc"] = [
            send(cx.at[k, :, :, theirs, cols], rc.at[k, :, :, :, cols], rs_s.at[q, 0], rs_r.at[q, 0], sibling)
        ]
        if o == 0:
            waits[q, "rc"].append(send(nrm.at[k], rcn.at[k], rs_s.at[q, 1], rs_r.at[q, 1], sibling))

    def reduce_y(q):
        k, o, n = parts[q]
        cols = pl.ds(o, n)
        for copy in waits[q, "rc"]:
            copy.wait_recv()
        pb[k, :, :, :, cols] = cx[k, :, :, mine, cols] + rc[k, :, :, :, cols]
        if o == 0:
            pn[k] = nrm[k] + rcn[k]
        waits[q, "ry"] = []
        for j in range(3):
            waits[q, "ry"].append(
                send(
                    pb.at[k, (y + j + 1) % YS, :, :, cols], ry.at[k, j, :, :, cols],
                    rs_s.at[q, 2 + j], rs_r.at[q, 2 + j], y_other[j],
                )
            )
            if o == 0:
                waits[q, "ry"].append(send(pn.at[k], ryn.at[k, j], rs_s.at[q, 5 + j], rs_r.at[q, 5 + j], y_other[j]))

    def reduce_z(q):
        k, o, n = parts[q]
        cols = pl.ds(o, n)
        for copy in waits[q, "ry"]:
            copy.wait_recv()
        get = lambda ref, j: ref[k, j, :, :, cols]
        qz[k, :, :, 128 + o : 128 + o + n] = get(pb, y) + get(ry, 0) + (get(ry, 1) + get(ry, 2))
        if o == 0:
            total = pn[k] + ryn[k, 0] + (ryn[k, 1] + ryn[k, 2])
            for j in range(ZS):
                qz[k, j, :, :128] = total
        with_norms = pl.ds(0, n + 128) if o == 0 else pl.ds(o + 128, n)
        waits[q, "rz"] = [
            send(
                qz.at[k, (z + j + 1) % ZS, :, with_norms], rz.at[k, j, :, with_norms],
                rs_s.at[q, 8 + j], rs_r.at[q, 8 + j], z_other[j],
            )
            for j in range(7)
        ]

    def couple(k):
        for q in range(3):
            if parts[q][0] == k:
                for copy in waits[q, "rz"]:
                    copy.wait_recv()
        total = qz[k, z]
        for j in range(7):
            total = total + rz[k, j]
        cross = total[:, 128:]
        norm = total[:, :128]
        rows = [jnp.concatenate([norm[4 * i + j : 4 * i + j + 1, :] for j in range(4)], axis=1) for i in range(2)]
        mean_top = rows[0] / TOTAL + 1e-06
        mean_bottom = rows[1] / TOTAL + 1e-06
        here = lax.broadcasted_iota(jnp.int32, (8, B), 0) + 8 * row
        column = lax.broadcasted_iota(jnp.int32, (8, B), 1)
        mean_top = jnp.sum(jnp.where(here == column, mean_top, 0.0), axis=1, keepdims=True)
        scale = jnp.sqrt(F32(TOTAL)) * jnp.sqrt(mean_top * mean_bottom)
        coup_ref[k, 0] = cross / scale

    def turn(k, high, low, o, n):
        w = rg[k, :, :, o : o + n].reshape(W, n)
        w_high, w_low = split(w)
        return dot3(high[...], low[...], w_high, w_low, ((1,), (0,)))

    plain = (pair != 3) & (pair != 4)
    tops_up = plain & (pair > 0) & (pair < PAIRS - 1)
    bottoms_down = plain & (pair > 0)

    def up(p, h):
        return pltpu.make_async_remote_copy(
            src_ref=staged.at[p], dst_ref=new.at[0, :, pl.ds(h * PART, PART)],
            send_sem=ms.at[p], recv_sem=mr.at[h, 0], device_id=after, device_id_type=MESH,
        )

    def down(p, h):
        return pltpu.make_async_remote_copy(
            src_ref=staged.at[p], dst_ref=new.at[1, :, pl.ds(h * PART, PART)],
            send_sem=ms.at[p], recv_sem=mr.at[h, 1], device_id=before, device_id_type=MESH,
        )

    def far(p, i, j):
        rows = pl.ds(*SHARES[j])
        return pltpu.make_async_remote_copy(
            src_ref=staged.at[p, rows],
            dst_ref=new.at[i, rows, pl.ds(p * PART, PART)] if j == 0 else passing.at[p, pl.ds(0, SHARES[j][1])],
            send_sem=cs.at[p, j], recv_sem=cr.at[p, 0] if j == 0 else pr.at[p],
            device_id=(row, 4 - i if j == 0 else (3 - j, 4 + j)[i]), device_id_type=MESH,
        )

    def passed(p, i, j):
        return pltpu.make_async_remote_copy(
            src_ref=passing.at[p, pl.ds(0, SHARES[j][1])], dst_ref=new.at[i, pl.ds(*SHARES[j]), pl.ds(p * PART, PART)],
            send_sem=ps.at[p], recv_sem=cr.at[p, j], device_id=(row, 4 - i), device_id_type=MESH,
        )

    def sends(p):
        i, h = p % 2, p // 2
        if p < 4:
            found = [(pair == 3 + k, [far(p, k, j) for j in (1, 2, 3, 0)]) for k in range(2)]
        else:
            found = [(pair == 3, [down(p, p - 4)]), (pair == 4, [up(p, p - 4)])]
        if i == 0:
            return found + [(tops_up, [up(p, h)])]
        return found + [(pair == 0, [up(p, h)]), (bottoms_down, [down(p, h)])]

    def move(p):
        for who, copies in sends(p):
            @pl.when(who)
            def _():
                for copy in copies:
                    copy.start()

        if p % 2 == 0:
            for k, at_pair in enumerate((0, PAIRS - 1)):
                @pl.when(pair == at_pair)
                def _():
                    new[k, :, p // 2 * PART : (p // 2 + 1) * PART] = staged[p]

    def sent(p):
        for who, copies in sends(p):
            @pl.when(who)
            def _():
                for copy in copies:
                    copy.wait_send()

        if p < 4:
            for i in range(2):
                for j in range(1, 4):
                    @pl.when(pair == (3 - j, 4 + j)[i])
                    def _():
                        passed(p, i, j).wait_send()

    def pass_on(p):
        for i in range(2):
            for j in range(1, 4):
                @pl.when(pair == (3 - j, 4 + j)[i])
                def _():
                    far(p, i, j).wait_recv()
                    passed(p, i, j).start()

    def arrived(h):
        @pl.when((pair > 0) & (pair != 4))
        def _():
            up(0, h).wait_recv()

        @pl.when((pair < PAIRS - 1) & (pair != 3))
        def _():
            down(0, h).wait_recv()

        for i in range(2):
            @pl.when(pair == 4 - i)
            def _():
                far(h, i, 0).wait_recv()
                for j in range(1, 4):
                    passed(h, i, j).wait_recv()

            into = slice(i * B + h * PART, i * B + (h + 1) * PART)
            block = new[i, :, h * PART : (h + 1) * PART]
            nh[:, into], nl[:, into] = split(block)
            nrm[1, 4 * i + h : 4 * i + h + 1, :] = jnp.sum(block * block, axis=0, keepdims=True)

    def first(u):
        gather_done(u)
        _, o, n = units[u]
        value = turn(0, xh, xl, o, n)
        for k in range(n // PART):
            staged[o // PART + k] = value[:, k * PART : (k + 1) * PART]
            move(o // PART + k)

    def second(g):
        out_ref[:, g * GROUP : (g + 1) * GROUP] = turn(1, nh, nl, g * GROUP, GROUP)

    gather_z1(0)
    gather_z1(1)
    gather_z1(2)
    x_copy.wait()
    xh[...], xl[...] = split(x_ref[...])
    norms()
    gram(0, xh, xl, 0, B)
    reduce_c(0)
    gather_z2(0)
    gather_z2(1)
    gather_z1(3)
    gather_z1(4)
    gather_z2(2)
    gather_y1(0)
    gather_y1(1)
    gather_z2(3)
    gather_y1(2)
    gather_z2(4)
    gather_z1(5)
    gather_z1(6)
    gather_c(0)
    gather_c(1)
    gather_y2(2)
    gather_y1(3)
    first(0)
    first(1)
    gather_y1(4)
    gather_c(2)
    gather_y2(3)
    pass_on(0)
    pass_on(1)
    gather_z2(5)
    first(2)
    gather_y2(4)
    reduce_y(0)
    gather_c(3)
    gather_z2(6)
    first(3)
    pass_on(2)
    pass_on(3)
    gather_c(4)
    first(4)
    gather_y1(5)
    arrived(0)
    arrived(1)
    gather_y1(6)
    arrived(2)
    arrived(3)
    gram(1, nh, nl, 0, GROUP)
    reduce_c(1)
    gram(1, nh, nl, GROUP, GROUP)
    reduce_c(2)
    reduce_y(1)
    reduce_y(2)
    gather_y2(5)
    gather_y2(6)
    reduce_z(0)
    reduce_z(1)
    reduce_z(2)
    gather_c(5)
    gather_c(6)
    gather_done(5)
    second(0)
    second(1)
    couple(0)
    gather_done(6)
    second(2)
    second(3)
    couple(1)
    for copy in pending:
        copy.wait_send()
    for p in range(8):
        sent(p)


def per_device(matrix, rotations):
    vmem = pl.BlockSpec(memory_space=pltpu.VMEM)
    scratch = [
        pltpu.VMEM((ROWS, W), F32),
        pltpu.VMEM((ROWS, W), BF16),
        pltpu.VMEM((ROWS, W), BF16),
        pltpu.VMEM((2, YS * ZS, CS * SHARE, W), F32),
        pltpu.VMEM((8, ROWS, PART), F32),
        pltpu.VMEM((2, ROWS, B), F32),
        pltpu.VMEM((ROWS, W), BF16),
        pltpu.VMEM((ROWS, W), BF16),
        pltpu.VMEM((2, YS, ZS, CS * 8, B), F32),
        pltpu.VMEM((2, 8, 128), F32),
        pltpu.VMEM((2, YS, ZS, 8, B), F32),
        pltpu.VMEM((2, 8, 128), F32),
        pltpu.VMEM((2, YS, ZS, 8, B), F32),
        pltpu.VMEM((2, 8, 128), F32),
        pltpu.VMEM((2, 3, ZS, 8, B), F32),
        pltpu.VMEM((2, 3, 8, 128), F32),
        pltpu.VMEM((2, ZS, 8, B + 128), F32),
        pltpu.VMEM((2, 7, 8, B + 128), F32),
        pltpu.VMEM((4, SHARES[0][1], PART), F32),
        pltpu.SemaphoreType.DMA,
        pltpu.SemaphoreType.DMA((7, 12)),
        pltpu.SemaphoreType.DMA((7, 12)),
        pltpu.SemaphoreType.DMA((8,)),
        pltpu.SemaphoreType.DMA((4, 2)),
        pltpu.SemaphoreType.DMA((3, 15)),
        pltpu.SemaphoreType.DMA((3, 15)),
        pltpu.SemaphoreType.DMA((4, 4)),
        pltpu.SemaphoreType.DMA((4, 4)),
        pltpu.SemaphoreType.DMA((4,)),
        pltpu.SemaphoreType.DMA((4,)),
    ]
    return pl.pallas_call(
        body,
        name="tournament",
        out_shape=(
            jax.ShapeDtypeStruct((ROWS, W), F32),
            jax.ShapeDtypeStruct((2, 1, 8, B), F32),
        ),
        in_specs=[pl.BlockSpec(memory_space=pl.ANY), vmem],
        out_specs=(vmem, vmem),
        scratch_shapes=scratch,
        compiler_params=pltpu.CompilerParams(
            collective_id=0, has_side_effects=True, vmem_limit_bytes=36 << 20
        ),
    )(matrix, rotations)


def solution(mesh):
    specs = (P("row", "pair"), P(None, "pair", "row", None))
    return jax.shard_map(
        per_device, mesh=mesh, in_specs=specs, out_specs=specs, check_vma=False
    )
```
